32 devices in a mesh: row: 8 (over y, x, core), col: 4 (over z).
Axes of the slice: x: 2, y: 2, z: 4, core: 2. Of those that a mesh axis runs over, the one named last changes fastest.
Arguments:
- amplitudes: bfloat16 [7168, 7168], P('row', 'col'), as said below
- integrals: bfloat16 [7168, 7168], P('row', 'col'), as said below
- occ_energy: float32 [80], replicated, may hold values from -2 to -0.5
- vir_energy: float32 [1000], replicated, may hold values from 0.5 to 4
- pair_occ: int32 [7168], replicated, may hold values from 0 to 79, as said below
- pair_vir: int32 [7168], replicated, may hold values from 0 to 999, as said below
Outputs:
- updated: float32 [7168, 7168], P('row', 'col')
The draws below stay inside these ranges and needn't reach their ends.
Inputs may be any that keep to these rules, and one draw needn't show every extreme that they name: amplitudes is exactly symmetric. integrals is exactly symmetric. pair_occ[p] mod 8 equals pair_vir[p] mod 8 (one irrep block), and no pair (pair_occ[p], pair_vir[p]) occurs twice. `pair_vir`: see pair_occ.
All inputs are finite; a program needn't handle non-finite values.
Results may differ from the reference program's by a relative error of at most 0.0003.
Values may be sent and summed in bfloat16 or wider, within the bound.
A program may use at most 192 MiB of HBM per device.

```python
import math
import jax
import jax.numpy as jnp

M = 7168
NOCC = 80
NVIR = 1000
NIRREP = 8


def symmetric_field(key):
    entries = jax.random.normal(key, (M, M), jnp.float32)
    return (entries + entries.T) * 0.7071


def draw_amplitudes(key, part):
    return symmetric_field(jax.random.fold_in(key, 11)).astype(jnp.bfloat16)


def draw_integrals(key, part):
    return (symmetric_field(jax.random.fold_in(key, 12)) * (1.0 / math.sqrt(M))).astype(jnp.bfloat16)


def pair_index(key):
    pair_count = NOCC * (NVIR // NIRREP)
    shuffled = jax.random.permutation(jax.random.fold_in(key, 7), jnp.arange(1, pair_count - 1, dtype=jnp.int32))[:M - 2]
    chosen = jnp.concatenate([jnp.array([0, pair_count - 1], dtype=jnp.int32), shuffled])
    return jax.random.permutation(jax.random.fold_in(key, 8), chosen)


def draw_pair_occ(key, part):
    return (pair_index(key) // (NVIR // NIRREP)).astype(jnp.int32)


def draw_pair_vir(key, part):
    indices = pair_index(key)
    occupied = indices // (NVIR // NIRREP)
    return (NIRREP * (indices % (NVIR // NIRREP)) + occupied % NIRREP).astype(jnp.int32)


def setup_inputs(seed: int = 0) -> dict:
    arg_keys = jax.random.split(jax.random.key(seed), 7)
    return {
        "amplitudes": draw_amplitudes(jax.random.fold_in(arg_keys[6], 71), 0),
        "integrals": draw_integrals(jax.random.fold_in(arg_keys[6], 71), 0),
        "occ_energy": jnp.clip(jax.random.uniform(arg_keys[2], (NOCC,), jnp.float32, -2.0, -0.5), -2.0, -0.5),
        "vir_energy": jnp.clip(jax.random.uniform(arg_keys[3], (NVIR,), jnp.float32, 0.5, 4.0), 0.5, 4.0),
        "pair_occ": draw_pair_occ(jax.random.fold_in(arg_keys[6], 71), 0),
        "pair_vir": draw_pair_vir(jax.random.fold_in(arg_keys[6], 71), 0),
    }


def reference(amplitudes, integrals, occ_energy, vir_energy, pair_occ, pair_vir):
    product = jnp.dot(amplitudes, integrals, preferred_element_type=jnp.float32)
    pair_gap = occ_energy[pair_occ] - vir_energy[pair_vir]
    return (product + product.T) / (pair_gap[:, None] + pair_gap[None, :])
```

```python
import jax
import jax.numpy as jnp
from jax import lax
from jax.sharding import PartitionSpec as P


def lookup(energies, orbital_index):
    labels = jnp.arange(energies.shape[0], dtype=jnp.int32)
    picked = jnp.where(orbital_index[:, None] == labels[None, :], energies[None, :], 0.0)
    return jnp.sum(picked, axis=1)


def arrivals(col, cols):
    order = []
    for hops in range(1, cols):
        if col >= hops:
            order.append((0, hops))
        if col + hops < cols:
            order.append((1, hops))
    return order


def chains(block, cols):
    held = {}
    up = down = block
    for hops in range(1, cols):
        up = lax.ppermute(up, "col", [(c, c + 1) for c in range(hops - 1, cols - 1)])
        down = lax.ppermute(down, "col", [(c, c - 1) for c in range(1, cols - hops + 1)])
        held[0, hops], held[1, hops] = up, down
    return held


def choose(held, sources, col):
    kinds = sorted(set(sources))
    picked = held[kinds[0]]
    for kind in kinds[1:]:
        wanted = jnp.zeros((), bool)
        for c, source in enumerate(sources):
            if source == kind:
                wanted = wanted | (col == c)
        picked = jnp.where(wanted, held[kind], picked)
    return picked


def shards_of(cols):
    orders = [arrivals(c, cols) for c in range(cols)]

    def shards(amplitudes, integrals, occ_energy, vir_energy, pair_occ, pair_vir):
        tile_rows, tile_cols = amplitudes.shape
        row, col = lax.axis_index("row"), lax.axis_index("col")
        amp_held = chains(amplitudes, cols)
        int_held = chains(integrals, cols)
        amp_panel = lax.all_gather(amplitudes, "row", axis=0, tiled=True)
        int_panel = lax.all_gather(integrals, "row", axis=0, tiled=True)

        row_occ = lax.dynamic_slice_in_dim(pair_occ, row * tile_rows, tile_rows)
        row_vir = lax.dynamic_slice_in_dim(pair_vir, row * tile_rows, tile_rows)
        col_occ = lax.dynamic_slice_in_dim(pair_occ, col * tile_cols, tile_cols)
        col_vir = lax.dynamic_slice_in_dim(pair_vir, col * tile_cols, tile_cols)
        row_gap = lookup(occ_energy, row_occ) - lookup(vir_energy, row_vir)
        col_gap = lookup(occ_energy, col_occ) - lookup(vir_energy, col_vir)

        def term(amp, integ, k):
            int_block = lax.dynamic_slice_in_dim(int_panel, k * tile_cols, tile_cols)
            amp_block = lax.dynamic_slice_in_dim(amp_panel, k * tile_cols, tile_cols)
            return jnp.dot(amp, int_block, preferred_element_type=jnp.float32) + jnp.dot(
                integ, amp_block, preferred_element_type=jnp.float32
            )

        total = term(amplitudes, integrals, col)
        for slot in range(cols - 1):
            sources = [order[slot] for order in orders]
            k = jnp.zeros((), jnp.int32)
            for c, (direction, hops) in enumerate(sources):
                k = jnp.where(col == c, c + hops if direction else c - hops, k)
            total = total + term(
                choose(amp_held, sources, col), choose(int_held, sources, col), k
            )
        return total / (row_gap[:, None] + col_gap[None, :])

    return shards


def solution(mesh):
    return jax.shard_map(
        shards_of(mesh.shape["col"]),
        mesh=mesh,
        in_specs=(P("row", "col"), P("row", "col"), P(), P(), P(), P()),
        out_specs=P("row", "col"),
        check_vma=False,
    )
```

```python
import jax
import jax.numpy as jnp
from jax import lax
from jax.experimental import pallas as pl
from jax.experimental.pallas import tpu as pltpu
from jax.sharding import PartitionSpec as P

CHUNKS = 14
MESH = pl.DeviceIdType.MESH


def lookup(energies, orbital_index):
    labels = jnp.arange(energies.shape[0], dtype=jnp.int32)
    picked = jnp.where(orbital_index[:, None] == labels[None, :], energies[None, :], 0.0)
    return jnp.sum(picked, axis=1)


def arrivals(col, cols):
    order = []
    for hops in range(1, cols):
        if col >= hops:
            order.append((0, hops))
        if col + hops < cols:
            order.append((1, hops))
    return order


def chains(block, cols):
    held = {}
    up = down = block
    for hops in range(1, cols):
        up = lax.ppermute(up, "col", [(c, c + 1) for c in range(hops - 1, cols - 1)])
        down = lax.ppermute(down, "col", [(c, c - 1) for c in range(1, cols - hops + 1)])
        held[0, hops], held[1, hops] = up, down
    return held


def choose(held, sources, col):
    kinds = sorted(set(sources))
    picked = held[kinds[0]]
    for kind in kinds[1:]:
        wanted = jnp.zeros((), bool)
        for c, source in enumerate(sources):
            if source == kind:
                wanted = wanted | (col == c)
        picked = jnp.where(wanted, held[kind], picked)
    return picked


def relays(n):
    if n == 4:
        upward = {(1, 0): 1, (2, 0): 2, (3, 0): 0, (2, 1): 1, (3, 1): 3, (3, 2): 2}
        downward = {(0, 1): 1, (0, 2): 0, (0, 3): 3, (1, 2): 2, (1, 3): 1, (2, 3): 2}
        return {**upward, **downward}
    chosen = {}
    for i in range(n):
        for j in range(n):
            low, high = min(i, j), max(i, j)
            near = 2 * (high - low) < n or (2 * (high - low) == n and low % 2 == 0)
            if i != j:
                chosen[i, j] = low if near else high
    return chosen


def swap_kernel(n, via, handed, product_ref, out_ref, relay_ref, send_sem, relay_sem, hand_sem, out_sem):
    row, col = lax.axis_index("row"), lax.axis_index("col")
    chip, core = row // 2, row % 2
    rows = out_ref.shape[1]
    step = rows // CHUNKS

    def look(table):
        value = jnp.int32(0)
        for (i, j), entry in table.items():
            value = jnp.where((chip == i) & (col == j), jnp.int32(entry), value)
        return value

    barrier = pltpu.get_barrier_semaphore()

    def greet(r, c):
        pl.semaphore_signal(barrier, inc=1, device_id=(r, c), device_id_type=MESH)

    def chunk(c):
        return pl.ds(pl.multiple_of(c * step, 8), step)

    @pl.when(chip != col)
    def _():
        there = look(via)
        back = look({(i, j): via[j, i] for i, j in via})
        slot = look({block: handed[l].index(block) for block, l in via.items()})
        for side in range(2):
            greet(2 * there + side, there)
            greet(2 * back + side, back)
        pl.semaphore_wait(barrier, 4)

        def copies(c):
            return [
                pltpu.make_async_remote_copy(
                    src_ref=product_ref.at[side, chunk(c)],
                    dst_ref=relay_ref.at[slot, core, chunk(c)],
                    send_sem=send_sem.at[side, c],
                    recv_sem=relay_sem.at[slot, core, c],
                    device_id=(2 * there + side, there),
                    device_id_type=MESH,
                )
                for side in range(2)
            ]

        def start(c, carry):
            for copy in copies(c):
                copy.start()
            return carry

        lax.fori_loop(0, CHUNKS, start, 0)

        def finish(c, carry):
            for half in range(2):
                part = out_ref.at[half, chunk(c)]
                pltpu.make_async_copy(part, part, out_sem.at[half, c]).wait()
            for copy in copies(c):
                copy.wait_send()
            return carry

        lax.fori_loop(0, CHUNKS, finish, 0)

    for l in range(n):
        @pl.when((chip == l) & (col == l))
        def _(l=l):
            blocks = handed[l]
            greet(2 * l + 1 - core, l)
            for i, j in blocks:
                for side in range(2):
                    greet(2 * i + side, j)
                    greet(2 * j + side, i)
            pl.semaphore_wait(barrier, 1 + 4 * len(blocks))

            across = pltpu.make_async_remote_copy(
                src_ref=product_ref.at[1 - core],
                dst_ref=out_ref.at[core],
                send_sem=send_sem.at[0, 0],
                recv_sem=out_sem.at[0, 0],
                device_id=(2 * l + 1 - core, l),
                device_id_type=MESH,
            )
            across.start()
            kept = pltpu.make_async_copy(product_ref.at[core], out_ref.at[core], send_sem.at[1, 0])
            kept.start()

            def hand(slot, half, c):
                i, j = blocks[slot]
                return pltpu.make_async_remote_copy(
                    src_ref=relay_ref.at[slot, half, chunk(c)],
                    dst_ref=out_ref.at[half, chunk(c)],
                    send_sem=hand_sem.at[slot, half, c],
                    recv_sem=out_sem.at[half, c],
                    device_id=(2 * j + core, i),
                    device_id_type=MESH,
                )

            def pass_on(c, carry):
                for slot in range(len(blocks)):
                    for half in range(2):
                        part = relay_ref.at[slot, half, chunk(c)]
                        pltpu.make_async_copy(part, part, relay_sem.at[slot, half, c]).wait()
                        hand(slot, half, c).start()
                return carry

            lax.fori_loop(0, CHUNKS, pass_on, 0)

            def finish(c, carry):
                for slot in range(len(blocks)):
                    for half in range(2):
                        hand(slot, half, c).wait_send()
                return carry

            lax.fori_loop(0, CHUNKS, finish, 0)
            kept.wait()
            across.wait()


def swap(product, n):
    via = relays(n)
    handed = [[block for block in via if via[block] == l] for l in range(n)]
    slots = max(len(blocks) for blocks in handed)
    anywhere = pl.BlockSpec(memory_space=pl.ANY)
    shape = product.shape
    return pl.pallas_call(
        lambda *refs: swap_kernel(n, via, handed, *refs),
        out_shape=(
            jax.ShapeDtypeStruct(shape, jnp.float32),
            jax.ShapeDtypeStruct((slots, *shape), jnp.float32),
        ),
        in_specs=[anywhere],
        out_specs=(anywhere, anywhere),
        scratch_shapes=[
            pltpu.SemaphoreType.DMA((2, CHUNKS)),
            pltpu.SemaphoreType.DMA((slots, 2, CHUNKS)),
            pltpu.SemaphoreType.DMA((slots, 2, CHUNKS)),
            pltpu.SemaphoreType.DMA((2, CHUNKS)),
        ],
        compiler_params=pltpu.CompilerParams(collective_id=0, has_side_effects=True),
    )(product)[0]


def shards_of(cols):
    orders = [arrivals(c, cols) for c in range(cols)]

    def shards(amplitudes, integrals, occ_energy, vir_energy, pair_occ, pair_vir):
        tile_rows, tile_cols = amplitudes.shape
        row, col = lax.axis_index("row"), lax.axis_index("col")
        amp_held = chains(amplitudes, cols)
        int_panel = lax.all_gather(integrals, "row", axis=0, tiled=True)

        row_occ = lax.dynamic_slice_in_dim(pair_occ, row * tile_rows, tile_rows)
        row_vir = lax.dynamic_slice_in_dim(pair_vir, row * tile_rows, tile_rows)
        col_occ = lax.dynamic_slice_in_dim(pair_occ, col * tile_cols, tile_cols)
        col_vir = lax.dynamic_slice_in_dim(pair_vir, col * tile_cols, tile_cols)
        row_gap = lookup(occ_energy, row_occ) - lookup(vir_energy, row_vir)
        col_gap = lookup(occ_energy, col_occ) - lookup(vir_energy, col_vir)

        def term(amp, k):
            int_block = lax.dynamic_slice_in_dim(int_panel, k * tile_cols, tile_cols)
            return jnp.dot(amp, int_block, preferred_element_type=jnp.float32)

        total = term(amplitudes, col)
        for slot in range(cols - 1):
            sources = [order[slot] for order in orders]
            k = jnp.zeros((), jnp.int32)
            for c, (direction, hops) in enumerate(sources):
                k = jnp.where(col == c, c + hops if direction else c - hops, k)
            total = total + term(choose(amp_held, sources, col), k)
        mirrored = swap(total.T.reshape(2, tile_rows, tile_rows), cols)
        mirrored = jnp.concatenate((mirrored[0], mirrored[1]), axis=1)
        return (total + mirrored) / (row_gap[:, None] + col_gap[None, :])

    return shards


def solution(mesh):
    return jax.shard_map(
        shards_of(mesh.shape["col"]),
        mesh=mesh,
        in_specs=(P("row", "col"), P("row", "col"), P(), P(), P(), P()),
        out_specs=P("row", "col"),
        check_vma=False,
    )
```

```python
import jax
import jax.numpy as jnp
from jax import lax
from jax.experimental import pallas as pl
from jax.experimental.pallas import tpu as pltpu
from jax.sharding import PartitionSpec as P

CHUNKS = 14
MESH = pl.DeviceIdType.MESH


def lookup(energies, orbital_index):
    labels = jnp.arange(energies.shape[0], dtype=jnp.int32)
    picked = jnp.where(orbital_index[:, None] == labels[None, :], energies[None, :], 0.0)
    return jnp.sum(picked, axis=1)


def arrivals(col, cols):
    order = []
    for hops in range(1, cols):
        if col >= hops:
            order.append((0, hops))
        if col + hops < cols:
            order.append((1, hops))
    return order


def chains(block, cols):
    held = {}
    up = down = block
    for hops in range(1, cols):
        up = lax.ppermute(up, "col", [(c, c + 1) for c in range(hops - 1, cols - 1)])
        down = lax.ppermute(down, "col", [(c, c - 1) for c in range(1, cols - hops + 1)])
        held[0, hops], held[1, hops] = up, down
    return held


def choose(held, sources, col):
    kinds = sorted(set(sources))
    picked = held[kinds[0]]
    for kind in kinds[1:]:
        wanted = jnp.zeros((), bool)
        for c, source in enumerate(sources):
            if source == kind:
                wanted = wanted | (col == c)
        picked = jnp.where(wanted, held[kind], picked)
    return picked


def relays(n):
    if n == 4:
        upward = {(1, 0): 1, (2, 0): 2, (3, 0): 0, (2, 1): 1, (3, 1): 3, (3, 2): 2}
        downward = {(0, 1): 1, (0, 2): 0, (0, 3): 3, (1, 2): 2, (1, 3): 1, (2, 3): 2}
        return {**upward, **downward}
    chosen = {}
    for i in range(n):
        for j in range(n):
            low, high = min(i, j), max(i, j)
            near = 2 * (high - low) < n or (2 * (high - low) == n and low % 2 == 0)
            if i != j:
                chosen[i, j] = low if near else high
    return chosen


def swap_kernel(n, via, handed, product_ref, out_ref, relay_ref, send_sem, relay_sem, hand_sem, out_sem):
    row, col = lax.axis_index("row"), lax.axis_index("col")
    chip, core = row // 2, row % 2
    rows = out_ref.shape[1]
    step = rows // CHUNKS

    def look(table):
        value = jnp.int32(0)
        for (i, j), entry in table.items():
            value = jnp.where((chip == i) & (col == j), jnp.int32(entry), value)
        return value

    barrier = pltpu.get_barrier_semaphore()

    def greet(r, c):
        pl.semaphore_signal(barrier, inc=1, device_id=(r, c), device_id_type=MESH)

    def chunk(c):
        return pl.ds(pl.multiple_of(c * step, 8), step)

    @pl.when(chip != col)
    def _():
        there = look(via)
        back = look({(i, j): via[j, i] for i, j in via})
        slot = look({block: handed[l].index(block) for block, l in via.items()})
        for side in range(2):
            greet(2 * there + side, there)
            greet(2 * back + side, back)
        pl.semaphore_wait(barrier, 4)

        def copies(c):
            return [
                pltpu.make_async_remote_copy(
                    src_ref=product_ref.at[side, chunk(c)],
                    dst_ref=relay_ref.at[slot, core, chunk(c)],
                    send_sem=send_sem.at[side, c],
                    recv_sem=relay_sem.at[slot, core, c],
                    device_id=(2 * there + side, there),
                    device_id_type=MESH,
                )
                for side in range(2)
            ]

        def start(c, carry):
            for copy in copies(c):
                copy.start()
            return carry

        lax.fori_loop(0, CHUNKS, start, 0)

        def finish(c, carry):
            for half in range(2):
                part = out_ref.at[half, chunk(c)]
                pltpu.make_async_copy(part, part, out_sem.at[half, c]).wait()
            for copy in copies(c):
                copy.wait_send()
            return carry

        lax.fori_loop(0, CHUNKS, finish, 0)

    for l in range(n):
        @pl.when((chip == l) & (col == l))
        def _(l=l):
            blocks = handed[l]
            greet(2 * l + 1 - core, l)
            for i, j in blocks:
                for side in range(2):
                    greet(2 * i + side, j)
                    greet(2 * j + side, i)
            pl.semaphore_wait(barrier, 1 + 4 * len(blocks))

            across = pltpu.make_async_remote_copy(
                src_ref=product_ref.at[1 - core],
                dst_ref=out_ref.at[core],
                send_sem=send_sem.at[0, 0],
                recv_sem=out_sem.at[0, 0],
                device_id=(2 * l + 1 - core, l),
                device_id_type=MESH,
            )
            across.start()
            kept = pltpu.make_async_copy(product_ref.at[core], out_ref.at[core], send_sem.at[1, 0])
            kept.start()

            def hand(slot, half, c):
                i, j = blocks[slot]
                return pltpu.make_async_remote_copy(
                    src_ref=relay_ref.at[slot, half, chunk(c)],
                    dst_ref=out_ref.at[half, chunk(c)],
                    send_sem=hand_sem.at[slot, half, c],
                    recv_sem=out_sem.at[half, c],
                    device_id=(2 * j + core, i),
                    device_id_type=MESH,
                )

            def pass_on(c, carry):
                for slot in range(len(blocks)):
                    for half in range(2):
                        part = relay_ref.at[slot, half, chunk(c)]
                        pltpu.make_async_copy(part, part, relay_sem.at[slot, half, c]).wait()
                        hand(slot, half, c).start()
                return carry

            lax.fori_loop(0, CHUNKS, pass_on, 0)

            def finish(c, carry):
                for slot in range(len(blocks)):
                    for half in range(2):
                        hand(slot, half, c).wait_send()
                return carry

            lax.fori_loop(0, CHUNKS, finish, 0)
            kept.wait()
            across.wait()


def swap(product, n):
    via = relays(n)
    handed = [[block for block in via if via[block] == l] for l in range(n)]
    slots = max(len(blocks) for blocks in handed)
    anywhere = pl.BlockSpec(memory_space=pl.ANY)
    shape = product.shape
    return pl.pallas_call(
        lambda *refs: swap_kernel(n, via, handed, *refs),
        out_shape=(
            jax.ShapeDtypeStruct(shape, jnp.float32),
            jax.ShapeDtypeStruct((slots, *shape), jnp.float32),
        ),
        in_specs=[anywhere],
        out_specs=(anywhere, anywhere),
        scratch_shapes=[
            pltpu.SemaphoreType.DMA((2, CHUNKS)),
            pltpu.SemaphoreType.DMA((slots, 2, CHUNKS)),
            pltpu.SemaphoreType.DMA((slots, 2, CHUNKS)),
            pltpu.SemaphoreType.DMA((2, CHUNKS)),
        ],
        compiler_params=pltpu.CompilerParams(collective_id=0, has_side_effects=True),
    )(product)[0]


def shards_of(cols):
    orders = [arrivals(c, cols) for c in range(cols)]

    def shards(amplitudes, integrals, occ_energy, vir_energy, pair_occ, pair_vir):
        tile_rows, tile_cols = amplitudes.shape
        row, col = lax.axis_index("row"), lax.axis_index("col")
        amp_held = chains(amplitudes, cols)
        int_panel = lax.all_gather(integrals, "row", axis=0, tiled=True)

        row_occ = lax.dynamic_slice_in_dim(pair_occ, row * tile_rows, tile_rows)
        row_vir = lax.dynamic_slice_in_dim(pair_vir, row * tile_rows, tile_rows)
        col_occ = lax.dynamic_slice_in_dim(pair_occ, col * tile_cols, tile_cols)
        col_vir = lax.dynamic_slice_in_dim(pair_vir, col * tile_cols, tile_cols)
        row_gap = lookup(occ_energy, row_occ) - lookup(vir_energy, row_vir)
        col_gap = lookup(occ_energy, col_occ) - lookup(vir_energy, col_vir)

        def term(amp, k):
            int_block = lax.dynamic_slice_in_dim(int_panel, k * tile_cols, tile_cols)
            return jnp.dot(amp, int_block, preferred_element_type=jnp.float32)

        total = term(amplitudes, col)
        for slot in range(cols - 1):
            sources = [order[slot] for order in orders]
            k = jnp.zeros((), jnp.int32)
            for c, (direction, hops) in enumerate(sources):
                k = jnp.where(col == c, c + hops if direction else c - hops, k)
            total = lax.optimization_barrier(total)
            total = total + term(choose(amp_held, sources, col), k)
        total = lax.optimization_barrier(total)
        mirrored = swap(total.T.reshape(2, tile_rows, tile_rows), cols)
        mirrored = jnp.concatenate((mirrored[0], mirrored[1]), axis=1)
        return (total + mirrored) / (row_gap[:, None] + col_gap[None, :])

    return shards


def solution(mesh):
    return jax.shard_map(
        shards_of(mesh.shape["col"]),
        mesh=mesh,
        in_specs=(P("row", "col"), P("row", "col"), P(), P(), P(), P()),
        out_specs=P("row", "col"),
        check_vma=False,
    )
```
